128 devices in a mesh: row: 8 (over x, core), col: 16 (over y, z).
Axes of the slice: x: 4, y: 4, z: 4, core: 2. Of those that a mesh axis runs over, the one named last changes fastest.
Arguments:
- amplitudes: float32 [256, 32768], P(('row', 'col')), may hold values from -6 to 6
- integrals: float32 [16384, 32768], P('row', 'col'), may hold values from -0.09375 to 0.09375
- ij_irrep: int32 [256], replicated, may hold values from 0 to 7
- ab_irrep: int32 [16384], P('row'), may hold values from 0 to 7
- cd_irrep: int32 [32768], P('col'), may hold values from 0 to 7
Outputs:
- ladder_out: float32 [256, 16384], P(('row', 'col'))
The draws below stay inside these ranges and needn't reach their ends.
All inputs are finite; a program needn't handle non-finite values.
Results may differ from the reference program's by a relative error of at most 0.000078.
Values sent between devices are 32-bit elements; how exact they have to be, the bound alone decides.
A program may use at most 64 MiB of HBM per device.

```python
import math
import jax
import jax.numpy as jnp
import numpy as np
from jax import lax

NOP = 256
NAB = 16384
NCD = 32768


def plant(array, rng, smallest, top_value):
    dims = array.shape
    spot = [jax.random.randint(jax.random.fold_in(rng, axis), (), 0, dims[axis]) for axis in range(len(dims))]
    array = array.at[tuple(spot)].set(smallest)
    longest = dims.index(max(dims))
    spot[longest] = (spot[longest] + 1) % dims[longest]
    return array.at[tuple(spot)].set(top_value)


def shard_levels(rng, dims, pieces, low, high):
    loudness, own = 1.0, jax.random.fold_in(rng, 6)
    for axis_at, parts in pieces:
        heights = jnp.exp(jax.random.uniform(jax.random.fold_in(own, axis_at), (parts,), jnp.float32, low / len(pieces), high / len(pieces)))
        loudness = loudness * jnp.repeat(heights, dims[axis_at] // parts).reshape([-1 if axis == axis_at else 1 for axis in range(len(dims))])
    return loudness


def rank_bounds(amount, skew):
    portions = [(1 << 20) // math.isqrt(rank ** skew) + 1 for rank in range(1, amount + 1)]
    spread = 1 + sum(portions) // (1 << 30)
    return np.cumsum(np.array([max(1, weight // spread) for weight in portions]))


def ranked_ids(own_key, shape, number_of, skew):
    grid = rank_bounds(number_of, skew)
    lot = jax.random.randint(jax.random.fold_in(own_key, 1), shape, 0, int(grid[number_of - 1]))
    grade = jnp.searchsorted(jnp.asarray(grid, jnp.int32), lot, side="right")
    return jax.random.permutation(jax.random.fold_in(own_key, 2), number_of)[grade].astype(jnp.int32)


def gaussian(stream_key, dims, scale, most, cuts=(), dtype=jnp.bfloat16):
    entries = jax.random.normal(stream_key, dims, jnp.float32) * scale
    if len(cuts) > 0:
        entries = shard_levels(stream_key, dims, cuts, -0.22, 0.18) * entries
    return jnp.clip(entries, min=-most, max=most).astype(dtype)


def setup_inputs(seed: int = 0) -> dict:
    splits = jax.random.split(jax.random.key(seed), 6)
    amplitudes = gaussian(splits[0], (NOP, NCD), 1.0, 6.0, ((0, 128),), jnp.float32)
    integrals = gaussian(splits[1], (NAB, NCD), (NCD // 8) ** -0.5, 0.09375, ((0, 8), (1, 16)), jnp.float32)
    ij_irrep = plant(jax.random.randint(splits[2], (NOP,), 0, 8), jax.random.fold_in(splits[2], 1), 0, 7).astype(jnp.int32)
    ab_irrep = plant(ranked_ids(splits[3], (NAB,), 8, 2), jax.random.fold_in(splits[3], 3), 0, 7).astype(jnp.int32)
    cd_irrep = plant(ranked_ids(splits[4], (NCD,), 8, 2), jax.random.fold_in(splits[4], 3), 0, 7).astype(jnp.int32)
    return {"amplitudes": amplitudes, "integrals": integrals, "ij_irrep": ij_irrep, "ab_irrep": ab_irrep, "cd_irrep": cd_irrep}


def reference(amplitudes, integrals, ij_irrep, ab_irrep, cd_irrep):
    masked_amps = jnp.where(cd_irrep[None, :] == ij_irrep[:, None], amplitudes, 0.0)
    ladder = lax.dot_general(masked_amps, integrals, (((1,), (1,)), ((), ())), precision=lax.Precision.HIGHEST, preferred_element_type=jnp.float32)
    return jnp.where(ab_irrep[None, :] == ij_irrep[:, None], ladder, 0.0)
```

```python
import functools

import jax
import jax.numpy as jnp
from jax import lax
from jax.experimental import pallas as pl
from jax.experimental.pallas import tpu as pltpu
from jax.sharding import PartitionSpec as P

MESH = pl.DeviceIdType.MESH
ROWS, COLS = 8, 16
NIJ = 256
CAP = 64
BLOCK = 2048
SUB = BLOCK // ROWS
CHUNKS = 8
CHUNK = BLOCK // CHUNKS
SHARE = BLOCK // COLS
F32, BF16 = jnp.float32, jnp.bfloat16
NT = (((1,), (1,)), ((), ()))


def dot(a, b, dims=(((1,), (0,)), ((), ()))):
    return lax.dot_general(a, b, dims, preferred_element_type=F32)


def halves(v):
    hi = v.astype(BF16)
    return hi, (v - hi.astype(F32)).astype(BF16)


def column(row):
    return jnp.transpose(jnp.broadcast_to(row, (128, 128)))


def remote(src, dst, send, recv, row, col):
    return pltpu.make_async_remote_copy(
        src_ref=src, dst_ref=dst, send_sem=send, recv_sem=recv, device_id=(row, col), device_id_type=MESH
    )


def kernel(
    amp_ref, int_ref, ij_ref, ab_ref, cd_ref, out_ref,
    ints, parts, ab_col, hop, mine, packed, gathered, weights, sums, got, fin, swapped,
    int_sem, local_sem, send, recv,
):
    r, c = lax.axis_index("row"), lax.axis_index("col")
    x, core = r // 2, r % 2
    sibling = x * 2 + 1 - core

    barrier = pltpu.get_barrier_semaphore()
    for t in range(1, ROWS):
        pl.semaphore_signal(barrier, inc=1, device_id=((r + t) % ROWS, c), device_id_type=MESH)
    for t in range(1, COLS):
        pl.semaphore_signal(barrier, inc=1, device_id=(r, (c + t) % COLS), device_id_type=MESH)

    def fetch(q):
        rows = pl.ds(q * CHUNK, CHUNK)
        return pltpu.make_async_copy(int_ref.at[rows], ints.at[rows], int_sem.at[q])

    for q in range(CHUNKS):
        fetch(q).start()

    ij_row = jnp.broadcast_to(ij_ref[...], (8, NIJ)).astype(F32).astype(BF16)
    source = lax.broadcasted_iota(jnp.int32, (NIJ, NIJ), 0)
    target = lax.broadcasted_iota(jnp.int32, (NIJ, NIJ), 1)
    wanted = jnp.where(target < 128, 2 * target, 2 * target - 255)
    reorder = jnp.where(source == wanted, 1.0, 0.0).astype(F32).astype(BF16)
    key_row = dot(ij_row, reorder)[0:1, :]
    key_col = [column(key_row[:, 0:128]), column(key_row[:, 128:256])]
    keys = jnp.concatenate(key_col, axis=0)
    keys = jnp.concatenate([keys, keys], axis=1)
    same = keys == key_row
    rank_row = jnp.sum(jnp.where(same & (source < target), 1.0, 0.0), axis=0, keepdims=True)
    rank_col = jnp.sum(jnp.where(same & (target < source), 1.0, 0.0), axis=1, keepdims=True)

    for q in range(COLS):
        ab_col[pl.ds(q * 128, 128), :] = column(ab_ref[:, pl.ds(q * 128, 128)])

    def prepare(first, last):
        for q in range(first, last):
            fetch(q).wait()

            def step(s, carry, q=q):
                rows = pl.ds(pl.multiple_of(q * CHUNK + s * 16, 16), 16)
                label = ab_col[rows, :]
                for j in range(BLOCK // 128):
                    lanes = pl.ds(j * 128, 128)
                    value = jnp.where(label == cd_ref[:, lanes], ints[rows, lanes], 0.0)
                    hi, lo = halves(value)
                    at = pl.ds(pl.multiple_of(s * 16, 16), 16)
                    parts[q, at, lanes] = hi
                    parts[q, pl.ds(pl.multiple_of(CHUNK + s * 16, 16), 16), lanes] = lo
                return carry

            lax.fori_loop(0, CHUNK // 16, step, 0)

    prepare(0, 3)
    pl.semaphore_wait(barrier, ROWS + COLS - 2)

    for t in range(1, ROWS):
        to = (r + t) % ROWS
        remote(amp_ref.at[:, to], hop.at[r], send.at[0], recv.at[0], to, c).start()
    own = pltpu.make_async_copy(amp_ref.at[:, r], hop.at[r], local_sem.at[0])
    own.start()
    prepare(3, 5)
    own.wait()
    drain = remote(hop.at[pl.ds(0, ROWS - 1)], hop.at[pl.ds(0, ROWS - 1)], send.at[0], recv.at[0], r, c)
    drain.wait_recv()
    for t in range(1, COLS):
        to = (c + t) % COLS
        remote(hop.at[:, to], mine.at[:, c], send.at[1], recv.at[1], r, to).start()
    own = pltpu.make_async_copy(hop.at[:, c], mine.at[:, c], local_sem.at[1])
    own.start()
    drain.wait_send()
    prepare(5, 7)
    own.wait()
    some = mine.at[:, pl.ds(0, COLS - 1)]
    drain = remote(some, some, send.at[1], recv.at[1], r, c)
    drain.wait_recv()

    slot = lax.broadcasted_iota(jnp.int32, (CAP, 128), 0).astype(F32)
    for t in range(2):
        cd_row = cd_ref[:, pl.ds(pl.multiple_of(r * SUB + t * 128, 128), 128)].astype(F32)
        total = jnp.zeros((CAP, 128), F32)
        for i in range(2):
            amps = mine[:, :, t * 2 + i, :].reshape(128, 128)
            amps = jnp.where(key_col[i] == cd_row, amps, 0.0)
            pick = jnp.where(rank_row[:, i * 128 : (i + 1) * 128] == slot, 1.0, 0.0).astype(BF16)
            hi, lo = halves(amps)
            total += dot(pick, hi) + dot(pick, lo)
        packed[:, t * 128 : (t + 1) * 128] = total
    drain.wait_send()

    remote(packed, gathered.at[r], send.at[2], recv.at[2], sibling, c).start()
    for t in (1, 3, 2):
        remote(packed, gathered.at[r], send.at[3], recv.at[3 + t], (x + t) % 4 * 2 + core, c).start()
    own = pltpu.make_async_copy(packed, gathered.at[r], local_sem.at[2])
    own.start()
    prepare(7, 8)
    own.wait()
    for t in (1, 3, 2):
        k = (x + 4 - t) % 4 * 2 + core
        remote(gathered.at[k], gathered.at[k], send.at[3], recv.at[3 + t], r, c).wait_recv()
        remote(gathered.at[k], gathered.at[k], send.at[7], recv.at[2], sibling, c).start()
    four = gathered.at[pl.ds(0, 4)]
    three = gathered.at[pl.ds(0, 3)]
    remote(four, four, send.at[2], recv.at[2], r, c).wait_recv()
    for k in range(ROWS):
        hi, lo = halves(gathered[k])
        weights[0:CAP, k * SUB : (k + 1) * SUB] = hi
        weights[CAP : 2 * CAP, k * SUB : (k + 1) * SUB] = lo

    lane = lax.broadcasted_iota(jnp.int32, (SHARE // 2, 128), 1)

    def chunk(j, carry):
        q = (c // 2 + 1 + j) % CHUNKS
        both = dot(parts[q], weights[...], NT)
        both = both[0:CHUNK] + both[CHUNK:]
        both = both + pltpu.roll(both, CAP, 1)
        for s in range(CHUNK // SHARE):
            to = q * 2 + s
            low = both[s * SHARE : s * SHARE + SHARE // 2]
            high = both[s * SHARE + SHARE // 2 : (s + 1) * SHARE]
            sums[to] = jnp.where(lane < CAP, low, high)

            @pl.when(to != c)
            def _():
                remote(sums.at[to], got.at[c], send.at[8], recv.at[8], r, to).start()

        return carry

    lax.fori_loop(0, CHUNKS, chunk, 0)
    own = pltpu.make_async_copy(sums.at[c], got.at[c], local_sem.at[3])
    own.start()
    own.wait()
    some = got.at[pl.ds(0, COLS - 1)]
    drain = remote(some, some, send.at[8], recv.at[8], r, c)
    drain.wait_recv()
    total = got[0]
    for k in range(1, COLS):
        total += got[k]

    ab_row = ab_ref[:, pl.ds(pl.multiple_of(c * SHARE, 128), SHARE)].astype(F32)
    hi, lo = halves(total)
    place = lax.broadcasted_iota(jnp.int32, (128, 128), 1).astype(F32)
    for i in range(2):
        rank = rank_col[i * 128 : (i + 1) * 128]
        pieces = []
        for h in range(2):
            pick = jnp.where(rank + float(h * CAP) == place, 1.0, 0.0).astype(BF16)
            pieces.append(dot(pick, hi, NT) + dot(pick, lo, NT))
        rows = jnp.concatenate(pieces, axis=1)
        fin[:, :, i, :] = jnp.where(key_col[i] == ab_row, rows, 0.0).reshape(ROWS, COLS, 128)
    drain.wait_send()

    for t in range(1, COLS):
        to = (c + t) % COLS
        remote(fin.at[:, to], swapped.at[:, c], send.at[9], recv.at[9], r, to).start()
    own = pltpu.make_async_copy(fin.at[:, c], swapped.at[:, c], local_sem.at[4])
    own.start()
    own.wait()
    some = swapped.at[:, pl.ds(0, COLS - 1)]
    drain = remote(some, some, send.at[9], recv.at[9], r, c)
    drain.wait_recv()
    for t in range(1, ROWS):
        to = (r + t) % ROWS
        remote(swapped.at[to], out_ref.at[r], send.at[10], recv.at[10], to, c).start()
    own = pltpu.make_async_copy(swapped.at[r], out_ref.at[r], local_sem.at[5])
    own.start()
    own.wait()
    drain.wait_send()
    some = out_ref.at[pl.ds(0, ROWS - 1)]
    drain = remote(some, some, send.at[10], recv.at[10], r, c)
    drain.wait_recv()
    drain.wait_send()
    remote(packed, packed, send.at[2], recv.at[2], r, c).wait_send()
    remote(three, three, send.at[3], recv.at[2], r, c).wait_send()
    remote(three, three, send.at[7], recv.at[2], r, c).wait_send()


def packed_body(amplitudes, integrals, ij_irrep, ab_irrep, cd_irrep):
    amps = amplitudes.reshape(2, COLS, ROWS, 2, 128).transpose(1, 2, 3, 0, 4).reshape(COLS, ROWS, 4, 128)
    vmem = pl.BlockSpec(memory_space=pltpu.VMEM)
    hbm = pl.BlockSpec(memory_space=pl.ANY)
    out = pl.pallas_call(
        kernel,
        out_shape=jax.ShapeDtypeStruct((ROWS, COLS, 2, 128), F32),
        in_specs=[hbm, hbm, vmem, vmem, vmem],
        out_specs=vmem,
        scratch_shapes=[
            pltpu.VMEM((BLOCK, BLOCK), F32),
            pltpu.VMEM((CHUNKS, 2 * CHUNK, BLOCK), BF16),
            pltpu.VMEM((BLOCK, 128), jnp.int32),
            pltpu.VMEM((ROWS, COLS, 4, 128), F32),
            pltpu.VMEM((ROWS, COLS, 4, 128), F32),
            pltpu.VMEM((CAP, SUB), F32),
            pltpu.VMEM((ROWS, CAP, SUB), F32),
            pltpu.VMEM((2 * CAP, BLOCK), BF16),
            pltpu.VMEM((COLS, SHARE // 2, 128), F32),
            pltpu.VMEM((COLS, SHARE // 2, 128), F32),
            pltpu.VMEM((ROWS, COLS, 2, 128), F32),
            pltpu.VMEM((ROWS, COLS, 2, 128), F32),
            pltpu.SemaphoreType.DMA((CHUNKS,)),
            pltpu.SemaphoreType.DMA((6,)),
            pltpu.SemaphoreType.DMA((11,)),
            pltpu.SemaphoreType.DMA((11,)),
        ],
        compiler_params=pltpu.CompilerParams(collective_id=0, has_side_effects=True, vmem_limit_bytes=58 << 20),
        name="packed_ladder",
    )(amps, integrals, ij_irrep.reshape(1, -1), ab_irrep.reshape(1, -1), cd_irrep.reshape(1, -1))
    return out.reshape(ROWS * COLS, 2, 128).transpose(1, 0, 2).reshape(2, ROWS * COLS * 128)


def plain_body(amplitudes, integrals, ij_irrep, ab_irrep, cd_irrep):
    by_column = lax.all_to_all(amplitudes, "col", split_axis=1, concat_axis=0, tiled=True)
    gathered = lax.all_gather(by_column, "row", axis=0, tiled=True)
    own_pairs = NIJ // (ROWS * COLS)
    ordered = gathered.reshape(ROWS, COLS, own_pairs, BLOCK).transpose(1, 0, 2, 3).reshape(NIJ, BLOCK)
    pair_irrep = ij_irrep.reshape(ROWS, COLS, own_pairs).transpose(1, 0, 2).reshape(NIJ)
    masked = jnp.where(cd_irrep[None, :] == pair_irrep[:, None], ordered, 0.0)
    product = lax.dot_general(
        masked, integrals, NT, precision=lax.Precision.HIGHEST, preferred_element_type=F32
    )
    product = jnp.where(pair_irrep[:, None] == ab_irrep[None, :], product, 0.0)
    shared = lax.psum_scatter(product, "col", scatter_dimension=0, tiled=True)
    return lax.all_to_all(shared, "row", split_axis=0, concat_axis=1, tiled=True)


def body(amplitudes, integrals, ij_irrep, ab_irrep, cd_irrep):
    sizes = jnp.sum(ij_irrep[None, :] == jnp.arange(8, dtype=jnp.int32)[:, None], axis=1)
    fits = jnp.max(sizes) <= CAP
    return lax.cond(fits, packed_body, plain_body, amplitudes, integrals, ij_irrep, ab_irrep, cd_irrep)


def solution(mesh):
    in_specs = (P(("row", "col"), None), P("row", "col"), P(), P("row"), P("col"))
    out_specs = P(("row", "col"), None)
    return jax.shard_map(body, mesh=mesh, in_specs=in_specs, out_specs=out_specs, check_vma=False)
```

```python
import functools

import jax
import jax.numpy as jnp
from jax import lax
from jax.experimental import pallas as pl
from jax.experimental.pallas import tpu as pltpu
from jax.sharding import PartitionSpec as P

MESH = pl.DeviceIdType.MESH
ROWS, COLS = 8, 16
NIJ = 256
CAP = 64
BLOCK = 2048
SUB = BLOCK // ROWS
CHUNKS = 8
CHUNK = BLOCK // CHUNKS
SHARE = BLOCK // COLS
F32, BF16 = jnp.float32, jnp.bfloat16
NT = (((1,), (1,)), ((), ()))


def dot(a, b, dims=(((1,), (0,)), ((), ()))):
    return lax.dot_general(a, b, dims, preferred_element_type=F32)


def halves(v):
    hi = v.astype(BF16)
    return hi, (v - hi.astype(F32)).astype(BF16)


def column(row):
    return jnp.transpose(jnp.broadcast_to(row, (128, 128)))


def remote(src, dst, send, recv, row, col):
    return pltpu.make_async_remote_copy(
        src_ref=src, dst_ref=dst, send_sem=send, recv_sem=recv, device_id=(row, col), device_id_type=MESH
    )


def kernel(
    base_ref, amp_ref, int_ref, ij_ref, ab_ref, cd_ref, out_ref, most_ref,
    ints, parts, ab_col, hop, mine, packed, gathered, sums, shares, got, fin, swapped,
    int_sem, local_sem, send, recv,
):
    r, c = lax.axis_index("row"), lax.axis_index("col")
    x, core = r // 2, r % 2
    sibling = x * 2 + 1 - core

    barrier = pltpu.get_barrier_semaphore()
    for t in range(1, ROWS):
        pl.semaphore_signal(barrier, inc=1, device_id=((r + t) % ROWS, c), device_id_type=MESH)
    for t in range(1, COLS):
        pl.semaphore_signal(barrier, inc=1, device_id=(r, (c + t) % COLS), device_id_type=MESH)

    def fetch(q):
        rows = pl.ds(q * CHUNK, CHUNK)
        return pltpu.make_async_copy(int_ref.at[rows], ints.at[rows], int_sem.at[q])

    for q in range(CHUNKS):
        fetch(q).start()

    ij_row = jnp.broadcast_to(ij_ref[...], (8, NIJ)).astype(F32).astype(BF16)
    source = lax.broadcasted_iota(jnp.int32, (NIJ, NIJ), 0)
    target = lax.broadcasted_iota(jnp.int32, (NIJ, NIJ), 1)
    wanted = jnp.where(target < 128, 2 * target, 2 * target - 255)
    reorder = jnp.where(source == wanted, 1.0, 0.0).astype(F32).astype(BF16)
    key_row = dot(ij_row, reorder)[0:1, :]
    key_col = [column(key_row[:, 0:128]), column(key_row[:, 128:256])]
    keys = jnp.concatenate(key_col, axis=0)
    keys = jnp.concatenate([keys, keys], axis=1)
    same = keys == key_row
    rank_row = jnp.sum(jnp.where(same & (source < target), 1.0, 0.0), axis=0, keepdims=True)
    rank_col = jnp.sum(jnp.where(same & (target < source), 1.0, 0.0), axis=1, keepdims=True)
    most_ref[...] = jnp.broadcast_to(jnp.max(rank_row, axis=1, keepdims=True) + 1.0, (8, 128)).astype(jnp.int32)
    base = base_ref[...].astype(F32)
    rank_row = rank_row - base[0:1, 0:1]
    rank_col = rank_col - base[0:1, 0:1]
    rank_col = jnp.where((rank_col >= 0.0) & (rank_col < float(CAP)), rank_col, -1.0 - 2 * CAP)

    for q in range(COLS):
        ab_col[pl.ds(q * 128, 128), :] = column(ab_ref[:, pl.ds(q * 128, 128)])

    def prepare(first, last):
        for q in range(first, last):
            fetch(q).wait()

            def step(s, carry, q=q):
                rows = pl.ds(pl.multiple_of(q * CHUNK + s * 16, 16), 16)
                label = ab_col[rows, :]
                for j in range(BLOCK // 128):
                    lanes = pl.ds(j * 128, 128)
                    value = jnp.where(label == cd_ref[:, lanes], ints[rows, lanes], 0.0)
                    hi, lo = halves(value)
                    at = pl.ds(pl.multiple_of(s * 16, 16), 16)
                    parts[q, at, lanes] = hi
                    parts[q, pl.ds(pl.multiple_of(CHUNK + s * 16, 16), 16), lanes] = lo
                return carry

            lax.fori_loop(0, CHUNK // 16, step, 0)

    prepare(0, 2)
    pl.semaphore_wait(barrier, ROWS + COLS - 2)

    for t in range(1, ROWS):
        to = (r + t) % ROWS
        remote(amp_ref.at[:, to], hop.at[r], send.at[0], recv.at[0], to, c).start()
    own = pltpu.make_async_copy(amp_ref.at[:, r], hop.at[r], local_sem.at[0])
    own.start()
    prepare(2, 5)
    own.wait()
    drain = remote(hop.at[pl.ds(0, ROWS - 1)], hop.at[pl.ds(0, ROWS - 1)], send.at[0], recv.at[0], r, c)
    drain.wait_recv()
    for t in range(1, COLS):
        to = (c + t) % COLS
        remote(hop.at[:, to], mine.at[:, c], send.at[1], recv.at[1], r, to).start()
    own = pltpu.make_async_copy(hop.at[:, c], mine.at[:, c], local_sem.at[1])
    own.start()
    drain.wait_send()
    prepare(5, 8)
    own.wait()
    some = mine.at[:, pl.ds(0, COLS - 1)]
    drain = remote(some, some, send.at[1], recv.at[1], r, c)
    drain.wait_recv()

    slot = lax.broadcasted_iota(jnp.int32, (CAP, 128), 0).astype(F32)
    for t in range(2):
        cd_row = cd_ref[:, pl.ds(pl.multiple_of(r * SUB + t * 128, 128), 128)].astype(F32)
        total = jnp.zeros((CAP, 128), F32)
        for i in range(2):
            amps = mine[:, :, t * 2 + i, :].reshape(128, 128)
            amps = jnp.where(key_col[i] == cd_row, amps, 0.0)
            pick = jnp.where(rank_row[:, i * 128 : (i + 1) * 128] == slot, 1.0, 0.0).astype(BF16)
            hi, lo = halves(amps)
            total += dot(pick, hi) + dot(pick, lo)
        packed[:, t * 128 : (t + 1) * 128] = total
    drain.wait_send()

    remote(packed, gathered.at[r], send.at[2], recv.at[2], sibling, c).start()
    for t in (1, 3, 2):
        remote(packed, gathered.at[r], send.at[3], recv.at[3 + t], (x + t) % 4 * 2 + core, c).start()

    def arrived(k, sem):
        remote(gathered.at[k], gathered.at[k], send.at[3], recv.at[sem], r, c).wait_recv()

    def forward(t):
        k = (x + 4 - t) % 4 * 2 + core
        arrived(k, 3 + t)
        remote(gathered.at[k], gathered.at[k], send.at[7], recv.at[10 + t], sibling, c).start()

    def accumulate(t, finish=None):
        chip = (x + 4 - t) % 4
        if t:
            arrived(chip * 2 + 1 - core, 10 + t)
            values = [gathered[chip * 2], gathered[chip * 2 + 1]]
        else:
            arrived(sibling, 2)
            own, other = packed[...], gathered[sibling]
            values = [jnp.where(core == 0, own, other), jnp.where(core == 0, other, own)]
        his, los = zip(*(halves(v) for v in values))
        weights = jnp.concatenate([jnp.concatenate(his, axis=1), jnp.concatenate(los, axis=1)], axis=0)
        lanes = pl.ds(pl.multiple_of(chip * 2 * SUB, 2 * SUB), 2 * SUB)
        for dy, dz in ((2, 1), (2, 0), (1, 1), (3, 1), (1, 0), (3, 0), (0, 1), (0, 0)):
            q = (c // 4 + dy) % 4 * 2 + (c % 4 // 2 + dz) % 2
            both = dot(parts[q, :, lanes], weights, NT)
            both = both[0:CHUNK] + both[CHUNK:]
            if t:
                both += sums[q]
            if finish is None:
                sums[q] = both
            else:
                finish(q, both)

    lane = lax.broadcasted_iota(jnp.int32, (SHARE // 2, 128), 1)

    def finish(q, both):
        both = both + pltpu.roll(both, CAP, 1)
        for s in range(CHUNK // SHARE):
            to = q * 2 + s
            low = both[s * SHARE : s * SHARE + SHARE // 2]
            high = both[s * SHARE + SHARE // 2 : (s + 1) * SHARE]
            shares[to] = jnp.where(lane < CAP, low, high)

            @pl.when(to != c)
            def _():
                remote(shares.at[to], got.at[c], send.at[8], recv.at[8], r, to).start()

    accumulate(0)
    forward(1)
    forward(3)
    accumulate(1)
    forward(2)
    accumulate(3)
    accumulate(2, finish)
    own = pltpu.make_async_copy(shares.at[c], got.at[c], local_sem.at[3])
    own.start()
    own.wait()
    some = got.at[pl.ds(0, COLS - 1)]
    drain = remote(some, some, send.at[8], recv.at[8], r, c)
    drain.wait_recv()
    total = got[0]
    for k in range(1, COLS):
        total += got[k]

    ab_row = ab_ref[:, pl.ds(pl.multiple_of(c * SHARE, 128), SHARE)].astype(F32)
    hi, lo = halves(total)
    place = lax.broadcasted_iota(jnp.int32, (128, 128), 1).astype(F32)
    for i in range(2):
        rank = rank_col[i * 128 : (i + 1) * 128]
        pieces = []
        for h in range(2):
            pick = jnp.where(rank + float(h * CAP) == place, 1.0, 0.0).astype(BF16)
            pieces.append(dot(pick, hi, NT) + dot(pick, lo, NT))
        rows = jnp.concatenate(pieces, axis=1)
        fin[:, :, i, :] = jnp.where(key_col[i] == ab_row, rows, 0.0).reshape(ROWS, COLS, 128)
    drain.wait_send()

    for t in range(1, COLS):
        to = (c + t) % COLS
        remote(fin.at[:, to], swapped.at[:, c], send.at[9], recv.at[9], r, to).start()
    own = pltpu.make_async_copy(fin.at[:, c], swapped.at[:, c], local_sem.at[4])
    own.start()
    own.wait()
    some = swapped.at[:, pl.ds(0, COLS - 1)]
    drain = remote(some, some, send.at[9], recv.at[9], r, c)
    drain.wait_recv()
    for t in range(1, ROWS):
        to = (r + t) % ROWS
        remote(swapped.at[to], out_ref.at[r], send.at[10], recv.at[10], to, c).start()
    own = pltpu.make_async_copy(swapped.at[r], out_ref.at[r], local_sem.at[5])
    own.start()
    own.wait()
    drain.wait_send()
    some = out_ref.at[pl.ds(0, ROWS - 1)]
    drain = remote(some, some, send.at[10], recv.at[10], r, c)
    drain.wait_recv()
    drain.wait_send()
    remote(packed, packed, send.at[2], recv.at[2], r, c).wait_send()
    three = gathered.at[pl.ds(0, 3)]
    remote(three, three, send.at[3], recv.at[2], r, c).wait_send()
    remote(three, three, send.at[7], recv.at[2], r, c).wait_send()


def packed_round(base, amps, integrals, ij_irrep, ab_irrep, cd_irrep):
    vmem = pl.BlockSpec(memory_space=pltpu.VMEM)
    hbm = pl.BlockSpec(memory_space=pl.ANY)
    out, most = pl.pallas_call(
        kernel,
        out_shape=(
            jax.ShapeDtypeStruct((ROWS, COLS, 2, 128), F32),
            jax.ShapeDtypeStruct((8, 128), jnp.int32),
        ),
        in_specs=[vmem, hbm, hbm, vmem, vmem, vmem],
        out_specs=(vmem, vmem),
        scratch_shapes=[
            pltpu.VMEM((BLOCK, BLOCK), F32),
            pltpu.VMEM((CHUNKS, 2 * CHUNK, BLOCK), BF16),
            pltpu.VMEM((BLOCK, 128), jnp.int32),
            pltpu.VMEM((ROWS, COLS, 4, 128), F32),
            pltpu.VMEM((ROWS, COLS, 4, 128), F32),
            pltpu.VMEM((CAP, SUB), F32),
            pltpu.VMEM((ROWS, CAP, SUB), F32),
            pltpu.VMEM((CHUNKS, CHUNK, 128), F32),
            pltpu.VMEM((COLS, SHARE // 2, 128), F32),
            pltpu.VMEM((COLS, SHARE // 2, 128), F32),
            pltpu.VMEM((ROWS, COLS, 2, 128), F32),
            pltpu.VMEM((ROWS, COLS, 2, 128), F32),
            pltpu.SemaphoreType.DMA((CHUNKS,)),
            pltpu.SemaphoreType.DMA((6,)),
            pltpu.SemaphoreType.DMA((14,)),
            pltpu.SemaphoreType.DMA((14,)),
        ],
        compiler_params=pltpu.CompilerParams(collective_id=0, has_side_effects=True, vmem_limit_bytes=58 << 20),
        name="packed_round",
    )(base, amps, integrals, ij_irrep, ab_irrep, cd_irrep)
    return out.reshape(ROWS * COLS, 2, 128).transpose(1, 0, 2).reshape(2, ROWS * COLS * 128), most


def body(amplitudes, integrals, ij_irrep, ab_irrep, cd_irrep):
    amps = amplitudes.reshape(2, COLS, ROWS, 2, 128).transpose(1, 2, 3, 0, 4).reshape(COLS, ROWS, 4, 128)
    rest = (amps, integrals, ij_irrep.reshape(1, -1), ab_irrep.reshape(1, -1), cd_irrep.reshape(1, -1))
    out, most = packed_round(jnp.zeros((1, 128), jnp.int32), *rest)

    def more(state):
        return state[0] < most[0, 0]

    def another(state):
        base, so_far = state
        return base + CAP, so_far + packed_round(jnp.full((1, 128), base, jnp.int32), *rest)[0]

    _, out = lax.while_loop(more, another, (jnp.int32(CAP), out))
    return out


def solution(mesh):
    in_specs = (P(("row", "col"), None), P("row", "col"), P(), P("row"), P("col"))
    out_specs = P(("row", "col"), None)
    return jax.shard_map(body, mesh=mesh, in_specs=in_specs, out_specs=out_specs, check_vma=False)
```

```python
import jax
import jax.numpy as jnp
import numpy as np
from jax import lax
from jax.experimental import pallas as pl
from jax.experimental.pallas import tpu as pltpu
from jax.sharding import PartitionSpec as P

MESH = pl.DeviceIdType.MESH
ROWS, COLS = 8, 16
XS = 4
NIJ = 256
HALF = NIJ // 2
CAP = 32
BLOCK = 2048
WIDE = BLOCK // XS
CHUNKS = 8
CHUNK = BLOCK // CHUNKS
SHARE = BLOCK // COLS
F32, BF16 = jnp.float32, jnp.bfloat16
NT = (((1,), (1,)), ((), ()))


def dot(a, b, dims=(((1,), (0,)), ((), ()))):
    return lax.dot_general(a, b, dims, preferred_element_type=F32)


def halves(v):
    hi = v.astype(BF16)
    return hi, (v - hi.astype(F32)).astype(BF16)


def column(row):
    return jnp.transpose(jnp.broadcast_to(row, (128, 128)))


def remote(src, dst, send, recv, row, col):
    return pltpu.make_async_remote_copy(
        src_ref=src, dst_ref=dst, send_sem=send, recv_sem=recv, device_id=(row, col), device_id_type=MESH
    )


def kernel(
    base_ref, amp_ref, int_ref, ij_ref, ab_ref, cd_ref, out_ref, most_ref,
    ints, parts, ab_col, mine, packed, gathered, sums, shares, got, fin,
    int_sem, local_sem, send, recv,
):
    r, c = lax.axis_index("row"), lax.axis_index("col")
    x, core = r // 2, r % 2
    sibling = x * 2 + 1 - core

    barrier = pltpu.get_barrier_semaphore()
    place_of = x * COLS + c
    pl.semaphore_signal(barrier, inc=1, device_id=(sibling, c), device_id_type=MESH)

    def greet(t, carry):
        peer = (place_of + t) % (XS * COLS)
        pl.semaphore_signal(barrier, inc=1, device_id=(peer // COLS * 2 + core, peer % COLS), device_id_type=MESH)
        return carry

    lax.fori_loop(1, XS * COLS, greet, 0)

    def fetch(q):
        rows = pl.ds(q * CHUNK, CHUNK)
        return pltpu.make_async_copy(int_ref.at[rows], ints.at[rows], int_sem.at[q])

    for q in range(CHUNKS):
        fetch(q).start()

    ij_row = jnp.broadcast_to(ij_ref[...], (8, NIJ)).astype(F32).astype(BF16)
    source = lax.broadcasted_iota(jnp.int32, (NIJ, NIJ), 0)
    target = lax.broadcasted_iota(jnp.int32, (NIJ, NIJ), 1)
    wanted = (target // 16 % 4) * 64 + (target // 128) * 32 + (target % 16) * 2 + (target // 64 % 2)
    reorder = jnp.where(source == wanted, 1.0, 0.0).astype(F32).astype(BF16)
    key_row = dot(ij_row, reorder)[0:1, :]
    key_col = [column(key_row[:, 0:HALF]), column(key_row[:, HALF:NIJ])]
    keys = jnp.concatenate(key_col, axis=0)
    keys = jnp.concatenate([keys, keys], axis=1)
    same = (keys == key_row) & (source // HALF == target // HALF)
    rank_row = jnp.sum(jnp.where(same & (source < target), 1.0, 0.0), axis=0, keepdims=True)
    rank_col = jnp.sum(jnp.where(same & (target < source), 1.0, 0.0), axis=1, keepdims=True)
    most_ref[...] = jnp.broadcast_to(jnp.max(rank_row, axis=1, keepdims=True) + 1.0, (8, 128)).astype(jnp.int32)
    base = base_ref[...].astype(F32)
    rank_row = rank_row - base[0:1, 0:1]
    rank_col = rank_col - base[0:1, 0:1]
    rank_col = jnp.where((rank_col >= 0.0) & (rank_col < float(CAP)), rank_col, -4.0 * NIJ)

    for q in range(COLS):
        ab_col[pl.ds(q * 128, 128), :] = column(ab_ref[:, pl.ds(q * 128, 128)])

    def prepare(first, last):
        for q in range(first, last):
            fetch(q).wait()

            def step(s, carry, q=q):
                rows = pl.ds(pl.multiple_of(q * CHUNK + s * 16, 16), 16)
                label = ab_col[rows, :]
                for j in range(BLOCK // 128):
                    lanes = pl.ds(j * 128, 128)
                    value = jnp.where(label == cd_ref[:, lanes], ints[rows, lanes], 0.0)
                    hi, lo = halves(value)
                    at = pl.ds(pl.multiple_of(s * 16, 16), 16)
                    parts[q, at, lanes] = hi
                    parts[q, pl.ds(pl.multiple_of(CHUNK + s * 16, 16), 16), lanes] = lo
                return carry

            lax.fori_loop(0, CHUNK // 16, step, 0)

    prepare(0, 3)
    pl.semaphore_wait(barrier, XS * COLS)

    def give(t, carry):
        peer = (place_of + t) % (XS * COLS)
        to_x, to_c = peer // COLS, peer % COLS
        remote(amp_ref.at[to_c, to_x], mine.at[place_of], send.at[0], recv.at[0], to_x * 2 + core, to_c).start()
        return carry

    lax.fori_loop(1, XS * COLS, give, 0)
    own = pltpu.make_async_copy(amp_ref.at[c, x], mine.at[place_of], local_sem.at[0])
    own.start()
    prepare(3, 8)
    own.wait()

    some = mine.at[pl.ds(0, XS * COLS - 1)]
    given = remote(some, some, send.at[0], recv.at[0], r, c)
    given.wait_recv()

    slot = lax.broadcasted_iota(jnp.int32, (CAP, HALF), 0).astype(F32)
    my_rank = jnp.where(core == 0, rank_row[:, 0:HALF], rank_row[:, HALF:NIJ])
    my_key = jnp.where(core == 0, key_col[0], key_col[1])
    pick = jnp.where(my_rank == slot, 1.0, 0.0).astype(BF16)
    for t in range(WIDE // 128):
        cd_row = cd_ref[:, pl.ds(pl.multiple_of(x * WIDE + t * 128, 128), 128)].astype(F32)
        amps = jnp.concatenate([mine[:, t * 2 + i, :] for i in range(2)], axis=0)
        hi, lo = halves(jnp.where(my_key == cd_row, amps, 0.0))
        packed[:, t * 128 : (t + 1) * 128] = dot(pick, hi) + dot(pick, lo)

    remote(packed, gathered.at[r], send.at[2], recv.at[2], sibling, c).start()
    for t in (1, 3, 2):
        remote(packed, gathered.at[r], send.at[3], recv.at[3 + t], (x + t) % 4 * 2 + core, c).start()

    def arrived(k, sem):
        remote(gathered.at[k], gathered.at[k], send.at[3], recv.at[sem], r, c).wait_recv()

    def forward(t):
        k = (x + 4 - t) % 4 * 2 + core
        arrived(k, 3 + t)
        remote(gathered.at[k], gathered.at[k], send.at[7], recv.at[10 + t], sibling, c).start()

    def accumulate(t, finish=None):
        chip = (x + 4 - t) % 4
        if t:
            arrived(chip * 2 + 1 - core, 10 + t)
            values = [gathered[chip * 2], gathered[chip * 2 + 1]]
        else:
            arrived(sibling, 2)
            own, other = packed[...], gathered[sibling]
            values = [jnp.where(core == 0, own, other), jnp.where(core == 0, other, own)]
        weights = jnp.concatenate(halves(jnp.concatenate(values, axis=0)), axis=0)
        lanes = pl.ds(pl.multiple_of(chip * WIDE, WIDE), WIDE)
        for dy, dz in ((2, 1), (2, 0), (1, 1), (3, 1), (1, 0), (3, 0), (0, 1), (0, 0)):
            q = (c // 4 + dy) % 4 * 2 + (c % 4 // 2 + dz) % 2
            both = dot(parts[q, :, lanes], weights, NT)
            both = both[0:CHUNK] + both[CHUNK:]
            if t:
                both += sums[q]
            if finish is None:
                sums[q] = both
            else:
                finish(q, both)

    lane = lax.broadcasted_iota(jnp.int32, (SHARE // 2, 128), 1)

    def finish(q, both):
        both = both + pltpu.roll(both, 2 * CAP, 1)
        for s in range(CHUNK // SHARE):
            to = q * 2 + s
            low = both[s * SHARE : s * SHARE + SHARE // 2]
            high = both[s * SHARE + SHARE // 2 : (s + 1) * SHARE]
            shares[to] = jnp.where(lane < 2 * CAP, low, high)

            @pl.when(to != c)
            def _():
                remote(shares.at[to], got.at[c], send.at[8], recv.at[8], r, to).start()

    accumulate(0)
    forward(1)
    forward(3)
    accumulate(1)
    forward(2)
    accumulate(3)
    accumulate(2, finish)
    own = pltpu.make_async_copy(shares.at[c], got.at[c], local_sem.at[3])
    own.start()
    own.wait()
    some = got.at[pl.ds(0, COLS - 1)]
    drain = remote(some, some, send.at[8], recv.at[8], r, c)
    drain.wait_recv()
    total = got[0]
    for k in range(1, COLS):
        total += got[k]

    ab_row = ab_ref[:, pl.ds(pl.multiple_of(c * SHARE, 128), SHARE)].astype(F32)
    hi, lo = halves(total)
    place = lax.broadcasted_iota(jnp.int32, (HALF, 128), 1).astype(F32)
    for g in range(2):
        slots = rank_col[g * HALF : (g + 1) * HALF] + float(g * CAP)
        pieces = []
        for h in range(2):
            pick = jnp.where(slots + float(h * 2 * CAP) == place, 1.0, 0.0).astype(BF16)
            pieces.append(dot(pick, hi, NT) + dot(pick, lo, NT))
        rows = jnp.where(key_col[g] == ab_row, jnp.concatenate(pieces, axis=1), 0.0)
        for i in range(2):
            fin[:, g, :, i, :] = rows[i * HALF // 2 : (i + 1) * HALF // 2].reshape(XS, COLS, 128)

    me = r * COLS + c

    def hand_out(t, carry):
        peer = (me + t) % (ROWS * COLS)
        to_r, to_c = peer // COLS, peer % COLS
        remote(fin.at[to_r // 2, to_r % 2, to_c], out_ref.at[me], send.at[9], recv.at[9], to_r, to_c).start()
        return carry

    lax.fori_loop(1, ROWS * COLS, hand_out, 0)
    own = pltpu.make_async_copy(fin.at[x, core, c], out_ref.at[me], local_sem.at[4])
    own.start()
    own.wait()
    drain.wait_send()
    some = out_ref.at[pl.ds(0, ROWS * COLS - 1)]
    handed = remote(some, some, send.at[9], recv.at[9], r, c)
    handed.wait_recv()
    handed.wait_send()
    given.wait_send()
    remote(packed, packed, send.at[2], recv.at[2], r, c).wait_send()
    three = gathered.at[pl.ds(0, 3)]
    remote(three, three, send.at[3], recv.at[2], r, c).wait_send()
    remote(three, three, send.at[7], recv.at[2], r, c).wait_send()


def packed_round(base, amps, integrals, ij_irrep, ab_irrep, cd_irrep):
    vmem = pl.BlockSpec(memory_space=pltpu.VMEM)
    hbm = pl.BlockSpec(memory_space=pl.ANY)
    out, most = pl.pallas_call(
        kernel,
        out_shape=(
            jax.ShapeDtypeStruct((ROWS * COLS, 2, 128), F32),
            jax.ShapeDtypeStruct((8, 128), jnp.int32),
        ),
        in_specs=[vmem, hbm, hbm, vmem, vmem, vmem],
        out_specs=(vmem, vmem),
        scratch_shapes=[
            pltpu.VMEM((BLOCK, BLOCK), F32),
            pltpu.VMEM((CHUNKS, 2 * CHUNK, BLOCK), BF16),
            pltpu.VMEM((BLOCK, 128), jnp.int32),
            pltpu.VMEM((XS * COLS, 8, 128), F32),
            pltpu.VMEM((CAP, WIDE), F32),
            pltpu.VMEM((ROWS, CAP, WIDE), F32),
            pltpu.VMEM((CHUNKS, CHUNK, 128), F32),
            pltpu.VMEM((COLS, SHARE // 2, 128), F32),
            pltpu.VMEM((COLS, SHARE // 2, 128), F32),
            pltpu.VMEM((XS, 2, COLS, 2, 128), F32),
            pltpu.SemaphoreType.DMA((CHUNKS,)),
            pltpu.SemaphoreType.DMA((6,)),
            pltpu.SemaphoreType.DMA((14,)),
            pltpu.SemaphoreType.DMA((14,)),
        ],
        compiler_params=pltpu.CompilerParams(collective_id=0, has_side_effects=True, vmem_limit_bytes=58 << 20),
        name="packed_round",
    )(base, amps, integrals, ij_irrep, ab_irrep, cd_irrep)
    return out.transpose(1, 0, 2).reshape(2, ROWS * COLS * 128), most


def body(amplitudes, integrals, ij_irrep, ab_irrep, cd_irrep):
    amps = amplitudes.reshape(2, COLS, XS, 4, 128).transpose(1, 2, 3, 0, 4).reshape(COLS, XS, 8, 128)
    rest = (amps, integrals, ij_irrep.reshape(1, -1), ab_irrep.reshape(1, -1), cd_irrep.reshape(1, -1))
    first = jnp.asarray(np.arange(128, dtype=np.int32)[None, :])
    out, most = packed_round(first, *rest)

    def more(state):
        return state[0] < most[0, 0]

    def another(state):
        base, so_far = state
        return base + CAP, so_far + packed_round(first + base, *rest)[0]

    _, out = lax.while_loop(more, another, (jnp.int32(CAP), out))
    return out


def solution(mesh):
    in_specs = (P(("row", "col"), None), P("row", "col"), P(), P("row"), P("col"))
    out_specs = P(("row", "col"), None)
    return jax.shard_map(body, mesh=mesh, in_specs=in_specs, out_specs=out_specs, check_vma=False)
```

```python
import jax
import jax.numpy as jnp
import numpy as np
from jax import lax
from jax.experimental import pallas as pl
from jax.experimental.pallas import tpu as pltpu
from jax.sharding import PartitionSpec as P

MESH = pl.DeviceIdType.MESH
ROWS, COLS = 8, 16
XS = 4
NIJ = 256
HALF = NIJ // 2
CAP = 32
BLOCK = 2048
WIDE = BLOCK // XS
CHUNKS = 8
CHUNK = BLOCK // CHUNKS
SHARE = BLOCK // COLS
F32, BF16 = jnp.float32, jnp.bfloat16
NT = (((1,), (1,)), ((), ()))


def dot(a, b, dims=(((1,), (0,)), ((), ()))):
    return lax.dot_general(a, b, dims, preferred_element_type=F32)


def halves(v):
    hi = v.astype(BF16)
    return hi, (v - hi.astype(F32)).astype(BF16)


def column(row):
    return jnp.transpose(jnp.broadcast_to(row, (128, 128)))


def remote(src, dst, send, recv, row, col):
    return pltpu.make_async_remote_copy(
        src_ref=src, dst_ref=dst, send_sem=send, recv_sem=recv, device_id=(row, col), device_id_type=MESH
    )


def kernel(
    base_ref, amp_ref, int_ref, ij_ref, ab_ref, cd_ref, out_ref, most_ref,
    ints, parts, ab_col, mine, packed, gathered, sums, shares, got, fin,
    int_sem, local_sem, send, recv,
):
    r, c = lax.axis_index("row"), lax.axis_index("col")
    x, core = r // 2, r % 2
    sibling = x * 2 + 1 - core

    def far_first(cores):
        near = lambda d: min(d, 4 - d)
        offsets = [(dx, dy, dz, dc) for dx in range(4) for dy in range(4) for dz in range(4) for dc in cores if dx or dy or dz or dc]
        return sorted(offsets, key=lambda o: -(near(o[0]) + near(o[1]) + near(o[2])))

    to_xs = [(x + d) % 4 for d in range(4)]
    to_ys = [(c // 4 + d) % 4 * 4 for d in range(4)]
    to_zs = [(c % 4 + d) % 4 for d in range(4)]
    to_cores = [core, 1 - core]

    barrier = pltpu.get_barrier_semaphore()
    place_of = x * COLS + c
    pl.semaphore_signal(barrier, inc=1, device_id=(sibling, c), device_id_type=MESH)

    for dx, dy, dz, dc in far_first((0,)):
        pl.semaphore_signal(barrier, inc=1, device_id=(to_xs[dx] * 2 + core, to_ys[dy] + to_zs[dz]), device_id_type=MESH)
    def fetch(q):
        rows = pl.ds(q * CHUNK, CHUNK)
        return pltpu.make_async_copy(int_ref.at[rows], ints.at[rows], int_sem.at[q])

    for q in range(CHUNKS):
        fetch(q).start()

    ij_row = jnp.broadcast_to(ij_ref[...], (8, NIJ)).astype(F32).astype(BF16)
    source = lax.broadcasted_iota(jnp.int32, (NIJ, NIJ), 0)
    target = lax.broadcasted_iota(jnp.int32, (NIJ, NIJ), 1)
    wanted = (target // 16 % 4) * 64 + (target // 128) * 32 + (target % 16) * 2 + (target // 64 % 2)
    reorder = jnp.where(source == wanted, 1.0, 0.0).astype(F32).astype(BF16)
    key_row = dot(ij_row, reorder)[0:1, :]
    key_col = [column(key_row[:, 0:HALF]), column(key_row[:, HALF:NIJ])]
    keys = jnp.concatenate(key_col, axis=0)
    keys = jnp.concatenate([keys, keys], axis=1)
    same = (keys == key_row) & (source // HALF == target // HALF)
    rank_row = jnp.sum(jnp.where(same & (source < target), 1.0, 0.0), axis=0, keepdims=True)
    rank_col = jnp.sum(jnp.where(same & (target < source), 1.0, 0.0), axis=1, keepdims=True)
    most_ref[0, 0] = jnp.max(rank_row).astype(jnp.int32) + 1
    base = base_ref[...].astype(F32)
    rank_row = rank_row - base[0:1, 0:1]
    rank_col = rank_col - base[0:1, 0:1]
    rank_col = jnp.where((rank_col >= 0.0) & (rank_col < float(CAP)), rank_col, -4.0 * NIJ)

    for q in range(COLS):
        ab_col[pl.ds(q * 128, 128), :] = column(ab_ref[:, pl.ds(q * 128, 128)])

    def prepare(first, last):
        for q in range(first, last):
            fetch(q).wait()

            def step(s, carry, q=q):
                rows = pl.ds(pl.multiple_of(q * CHUNK + s * 16, 16), 16)
                label = ab_col[rows, :]
                for j in range(BLOCK // 128):
                    lanes = pl.ds(j * 128, 128)
                    value = jnp.where(label == cd_ref[:, lanes], ints[rows, lanes], 0.0)
                    hi, lo = halves(value)
                    at = pl.ds(pl.multiple_of(s * 16, 16), 16)
                    parts[q, at, lanes] = hi
                    parts[q, pl.ds(pl.multiple_of(CHUNK + s * 16, 16), 16), lanes] = lo
                return carry

            lax.fori_loop(0, CHUNK // 16, step, 0)

    prepare(0, 3)
    pl.semaphore_wait(barrier, XS * COLS)

    for dx, dy, dz, dc in far_first((0,)):
        to_x, to_c = to_xs[dx], to_ys[dy] + to_zs[dz]
        remote(amp_ref.at[to_c, to_x], mine.at[place_of], send.at[0], recv.at[0], to_x * 2 + core, to_c).start()
    own = pltpu.make_async_copy(amp_ref.at[c, x], mine.at[place_of], local_sem.at[0])
    own.start()
    prepare(3, 8)
    own.wait()

    some = mine.at[pl.ds(0, XS * COLS - 1)]
    given = remote(some, some, send.at[0], recv.at[0], r, c)
    given.wait_recv()

    slot = lax.broadcasted_iota(jnp.int32, (CAP, HALF), 0).astype(F32)
    my_rank = jnp.where(core == 0, rank_row[:, 0:HALF], rank_row[:, HALF:NIJ])
    my_key = jnp.where(core == 0, key_col[0], key_col[1])
    pick = jnp.where(my_rank == slot, 1.0, 0.0).astype(BF16)
    for t in range(WIDE // 128):
        cd_row = cd_ref[:, pl.ds(pl.multiple_of(x * WIDE + t * 128, 128), 128)].astype(F32)
        amps = jnp.concatenate([mine[:, t * 2 + i, :] for i in range(2)], axis=0)
        hi, lo = halves(jnp.where(my_key == cd_row, amps, 0.0))
        packed[:, t * 128 : (t + 1) * 128] = dot(pick, hi) + dot(pick, lo)

    remote(packed, gathered.at[r], send.at[2], recv.at[2], sibling, c).start()
    for t in (1, 3, 2):
        remote(packed, gathered.at[r], send.at[3], recv.at[3 + t], (x + t) % 4 * 2 + core, c).start()

    def arrived(k, sem):
        remote(gathered.at[k], gathered.at[k], send.at[3], recv.at[sem], r, c).wait_recv()

    def forward(t):
        k = (x + 4 - t) % 4 * 2 + core
        arrived(k, 3 + t)
        remote(gathered.at[k], gathered.at[k], send.at[7], recv.at[10 + t], sibling, c).start()

    def accumulate(t, finish=None):
        chip = (x + 4 - t) % 4
        if t:
            arrived(chip * 2 + 1 - core, 10 + t)
            values = [gathered[chip * 2], gathered[chip * 2 + 1]]
        else:
            arrived(sibling, 2)
            own, other = packed[...], gathered[sibling]
            values = [jnp.where(core == 0, own, other), jnp.where(core == 0, other, own)]
        weights = jnp.concatenate(halves(jnp.concatenate(values, axis=0)), axis=0)
        lanes = pl.ds(pl.multiple_of(chip * WIDE, WIDE), WIDE)
        for dy, dz in ((2, 1), (2, 0), (1, 1), (3, 1), (1, 0), (3, 0), (0, 1), (0, 0)):
            q = (c // 4 + dy) % 4 * 2 + (c % 4 // 2 + dz) % 2
            both = dot(parts[q, :, lanes], weights, NT)
            both = both[0:CHUNK] + both[CHUNK:]
            if t:
                both += sums[q]
            if finish is None:
                sums[q] = both
            else:
                finish(q, both)

    lane = lax.broadcasted_iota(jnp.int32, (SHARE // 2, 128), 1)

    def finish(q, both):
        both = both + pltpu.roll(both, 2 * CAP, 1)
        for s in range(CHUNK // SHARE):
            to = q * 2 + s
            low = both[s * SHARE : s * SHARE + SHARE // 2]
            high = both[s * SHARE + SHARE // 2 : (s + 1) * SHARE]
            shares[to] = jnp.where(lane < 2 * CAP, low, high)

            @pl.when(to != c)
            def _():
                remote(shares.at[to], got.at[c], send.at[8], recv.at[8], r, to).start()

    accumulate(0)
    forward(1)
    forward(3)
    accumulate(1)
    forward(2)
    accumulate(3)
    accumulate(2, finish)
    own = pltpu.make_async_copy(shares.at[c], got.at[c], local_sem.at[3])
    own.start()
    own.wait()
    some = got.at[pl.ds(0, COLS - 1)]
    drain = remote(some, some, send.at[8], recv.at[8], r, c)
    drain.wait_recv()
    total = got[0]
    for k in range(1, COLS):
        total += got[k]

    ab_row = ab_ref[:, pl.ds(pl.multiple_of(c * SHARE, 128), SHARE)].astype(F32)
    hi, lo = halves(total)
    place = lax.broadcasted_iota(jnp.int32, (HALF, 128), 1).astype(F32)
    for g in range(2):
        slots = rank_col[g * HALF : (g + 1) * HALF] + float(g * CAP)
        pieces = []
        for h in range(2):
            pick = jnp.where(slots + float(h * 2 * CAP) == place, 1.0, 0.0).astype(BF16)
            pieces.append(dot(pick, hi, NT) + dot(pick, lo, NT))
        rows = jnp.where(key_col[g] == ab_row, jnp.concatenate(pieces, axis=1), 0.0)
        for i in range(2):
            fin[:, g, :, i, :] = rows[i * HALF // 2 : (i + 1) * HALF // 2].reshape(XS, COLS, 128)

    me = r * COLS + c

    for dx, dy, dz, dc in far_first((0, 1)):
        to_x, to_c, to_core = to_xs[dx], to_ys[dy] + to_zs[dz], to_cores[dc]
        remote(fin.at[to_x, to_core, to_c], out_ref.at[me], send.at[9], recv.at[9], to_x * 2 + to_core, to_c).start()
    own = pltpu.make_async_copy(fin.at[x, core, c], out_ref.at[me], local_sem.at[4])
    own.start()
    own.wait()
    drain.wait_send()
    some = out_ref.at[pl.ds(0, ROWS * COLS - 1)]
    handed = remote(some, some, send.at[9], recv.at[9], r, c)
    handed.wait_recv()
    handed.wait_send()
    given.wait_send()
    remote(packed, packed, send.at[2], recv.at[2], r, c).wait_send()
    three = gathered.at[pl.ds(0, 3)]
    remote(three, three, send.at[3], recv.at[2], r, c).wait_send()
    remote(three, three, send.at[7], recv.at[2], r, c).wait_send()


def packed_round(base, amps, integrals, ij_irrep, ab_irrep, cd_irrep):
    vmem = pl.BlockSpec(memory_space=pltpu.VMEM)
    hbm = pl.BlockSpec(memory_space=pl.ANY)
    out, most = pl.pallas_call(
        kernel,
        out_shape=(
            jax.ShapeDtypeStruct((ROWS * COLS, 2, 128), F32),
            jax.ShapeDtypeStruct((1, 1), jnp.int32),
        ),
        in_specs=[vmem, hbm, hbm, vmem, vmem, vmem],
        out_specs=(vmem, pl.BlockSpec(memory_space=pltpu.SMEM)),
        scratch_shapes=[
            pltpu.VMEM((BLOCK, BLOCK), F32),
            pltpu.VMEM((CHUNKS, 2 * CHUNK, BLOCK), BF16),
            pltpu.VMEM((BLOCK, 128), jnp.int32),
            pltpu.VMEM((XS * COLS, 8, 128), F32),
            pltpu.VMEM((CAP, WIDE), F32),
            pltpu.VMEM((ROWS, CAP, WIDE), F32),
            pltpu.VMEM((CHUNKS, CHUNK, 128), F32),
            pltpu.VMEM((COLS, SHARE // 2, 128), F32),
            pltpu.VMEM((COLS, SHARE // 2, 128), F32),
            pltpu.VMEM((XS, 2, COLS, 2, 128), F32),
            pltpu.SemaphoreType.DMA((CHUNKS,)),
            pltpu.SemaphoreType.DMA((6,)),
            pltpu.SemaphoreType.DMA((14,)),
            pltpu.SemaphoreType.DMA((14,)),
        ],
        compiler_params=pltpu.CompilerParams(collective_id=0, has_side_effects=True, vmem_limit_bytes=58 << 20),
        name="packed_round",
    )(base, amps, integrals, ij_irrep, ab_irrep, cd_irrep)
    return out.transpose(1, 0, 2).reshape(2, ROWS * COLS * 128), most


def body(amplitudes, integrals, ij_irrep, ab_irrep, cd_irrep):
    amps = amplitudes.reshape(2, COLS, XS, 4, 128).transpose(1, 2, 3, 0, 4).reshape(COLS, XS, 8, 128)
    rest = (amps, integrals, ij_irrep.reshape(1, -1), ab_irrep.reshape(1, -1), cd_irrep.reshape(1, -1))
    first = jnp.asarray(np.arange(128, dtype=np.int32)[None, :])
    out, most = packed_round(first, *rest)

    def more(state):
        return state[0] < most[0, 0]

    def another(state):
        base, so_far = state
        return base + CAP, so_far + packed_round(first + base, *rest)[0]

    _, out = lax.while_loop(more, another, (jnp.int32(CAP), out))
    return out


def solution(mesh):
    in_specs = (P(("row", "col"), None), P("row", "col"), P(), P("row"), P("col"))
    out_specs = P(("row", "col"), None)
    return jax.shard_map(body, mesh=mesh, in_specs=in_specs, out_specs=out_specs, check_vma=False)
```

```python
import jax
import jax.numpy as jnp
import numpy as np
from jax import lax
from jax.experimental import pallas as pl
from jax.experimental.pallas import tpu as pltpu
from jax.sharding import PartitionSpec as P

MESH = pl.DeviceIdType.MESH
ROWS, COLS = 8, 16
XS = 4
NIJ = 256
HALF = NIJ // 2
CAP = 32
BLOCK = 2048
WIDE = BLOCK // XS
CHUNKS = 8
CHUNK = BLOCK // CHUNKS
SHARE = BLOCK // COLS
F32, BF16 = jnp.float32, jnp.bfloat16
NT = (((1,), (1,)), ((), ()))


def dot(a, b, dims=(((1,), (0,)), ((), ()))):
    return lax.dot_general(a, b, dims, preferred_element_type=F32)


def halves(v):
    hi = v.astype(BF16)
    return hi, (v - hi.astype(F32)).astype(BF16)


def column(row):
    return jnp.transpose(jnp.broadcast_to(row, (128, 128)))


def remote(src, dst, send, recv, row, col):
    return pltpu.make_async_remote_copy(
        src_ref=src, dst_ref=dst, send_sem=send, recv_sem=recv, device_id=(row, col), device_id_type=MESH
    )


def kernel(
    base_ref, amp_ref, int_ref, ij_ref, ab_ref, cd_ref, out_ref, most_ref,
    ints, parts, ab_col, mine, packed, gathered, sums, shares, got, fin,
    int_sem, local_sem, send, recv,
):
    r, c = lax.axis_index("row"), lax.axis_index("col")
    x, core = r // 2, r % 2
    sibling = x * 2 + 1 - core

    def far_first(cores):
        near = lambda d: min(d, 4 - d)
        offsets = [(dx, dy, dz, dc) for dx in range(4) for dy in range(4) for dz in range(4) for dc in cores if dx or dy or dz or dc]
        return sorted(offsets, key=lambda o: -(near(o[0]) + near(o[1]) + near(o[2])))

    to_xs = [(x + d) % 4 for d in range(4)]
    to_ys = [(c // 4 + d) % 4 * 4 for d in range(4)]
    to_zs = [(c % 4 + d) % 4 for d in range(4)]
    to_cores = [core, 1 - core]

    barrier = pltpu.get_barrier_semaphore()
    place_of = x * COLS + c
    pl.semaphore_signal(barrier, inc=1, device_id=(sibling, c), device_id_type=MESH)

    for dx, dy, dz, dc in far_first((0,)):
        pl.semaphore_signal(barrier, inc=1, device_id=(to_xs[dx] * 2 + core, to_ys[dy] + to_zs[dz]), device_id_type=MESH)
    def fetch(q):
        rows = pl.ds(q * CHUNK, CHUNK)
        return pltpu.make_async_copy(int_ref.at[rows], ints.at[rows], int_sem.at[q])

    for q in range(CHUNKS):
        fetch(q).start()

    ij_row = jnp.broadcast_to(ij_ref[...], (8, NIJ)).astype(F32).astype(BF16)
    source = lax.broadcasted_iota(jnp.int32, (NIJ, NIJ), 0)
    target = lax.broadcasted_iota(jnp.int32, (NIJ, NIJ), 1)
    wanted = (target // 16 % 4) * 64 + (target // 128) * 32 + (target % 16) * 2 + (target // 64 % 2)
    reorder = jnp.where(source == wanted, 1.0, 0.0).astype(F32).astype(BF16)
    key_row = dot(ij_row, reorder)[0:1, :]
    key_col = [column(key_row[:, 0:HALF]), column(key_row[:, HALF:NIJ])]
    keys = jnp.concatenate(key_col, axis=0)
    keys = jnp.concatenate([keys, keys], axis=1)
    same = (keys == key_row) & (source // HALF == target // HALF)
    rank_row = jnp.sum(jnp.where(same & (source < target), 1.0, 0.0), axis=0, keepdims=True)
    rank_col = jnp.sum(jnp.where(same & (target < source), 1.0, 0.0), axis=1, keepdims=True)
    most_ref[0, 0] = jnp.max(rank_row).astype(jnp.int32) + 1
    base = base_ref[...].astype(F32)
    rank_row = rank_row - base[0:1, 0:1]
    rank_col = rank_col - base[0:1, 0:1]
    rank_col = jnp.where((rank_col >= 0.0) & (rank_col < float(CAP)), rank_col, -4.0 * NIJ)

    for q in range(COLS):
        ab_col[pl.ds(q * 128, 128), :] = column(ab_ref[:, pl.ds(q * 128, 128)])

    def prepare(first, last):
        for q in range(first, last):
            fetch(q).wait()

            def step(s, carry, q=q):
                rows = pl.ds(pl.multiple_of(q * CHUNK + s * 16, 16), 16)
                label = ab_col[rows, :]
                for j in range(BLOCK // 128):
                    lanes = pl.ds(j * 128, 128)
                    value = jnp.where(label == cd_ref[:, lanes], ints[rows, lanes], 0.0)
                    hi, lo = halves(value)
                    at = pl.ds(pl.multiple_of(s * 16, 16), 16)
                    parts[q, at, lanes] = hi
                    parts[q, pl.ds(pl.multiple_of(CHUNK + s * 16, 16), 16), lanes] = lo
                return carry

            lax.fori_loop(0, CHUNK // 16, step, 0)

    prepare(0, 2)
    pl.semaphore_wait(barrier, XS * COLS)

    for dx, dy, dz, dc in far_first((0,)):
        to_x, to_c = to_xs[dx], to_ys[dy] + to_zs[dz]
        remote(amp_ref.at[to_c, to_x], mine.at[place_of], send.at[0], recv.at[0], to_x * 2 + core, to_c).start()
    own = pltpu.make_async_copy(amp_ref.at[c, x], mine.at[place_of], local_sem.at[0])
    own.start()
    prepare(2, 8)
    own.wait()

    some = mine.at[pl.ds(0, XS * COLS - 1)]
    given = remote(some, some, send.at[0], recv.at[0], r, c)
    given.wait_recv()

    slot = lax.broadcasted_iota(jnp.int32, (CAP, HALF), 0).astype(F32)
    my_rank = jnp.where(core == 0, rank_row[:, 0:HALF], rank_row[:, HALF:NIJ])
    my_key = jnp.where(core == 0, key_col[0], key_col[1])
    pick = jnp.where(my_rank == slot, 1.0, 0.0).astype(BF16)
    for t in range(WIDE // 128):
        cd_row = cd_ref[:, pl.ds(pl.multiple_of(x * WIDE + t * 128, 128), 128)].astype(F32)
        amps = jnp.concatenate([mine[:, t * 2 + i, :] for i in range(2)], axis=0)
        hi, lo = halves(jnp.where(my_key == cd_row, amps, 0.0))
        packed[:, t * 128 : (t + 1) * 128] = dot(pick, hi) + dot(pick, lo)

    for t in (1, 3, 2):
        remote(packed, gathered.at[r], send.at[3], recv.at[3 + t], (x + t) % 4 * 2 + core, c).start()
    remote(packed, gathered.at[r], send.at[2], recv.at[2], sibling, c).start()

    def arrived(k, sem):
        remote(gathered.at[k], gathered.at[k], send.at[3], recv.at[sem], r, c).wait_recv()

    def forward(t):
        k = (x + 4 - t) % 4 * 2 + core
        arrived(k, 3 + t)
        remote(gathered.at[k], gathered.at[k], send.at[7], recv.at[10 + t], sibling, c).start()

    def accumulate(t, finish=None):
        chip = (x + 4 - t) % 4
        if t:
            arrived(chip * 2 + 1 - core, 10 + t)
            values = [gathered[chip * 2], gathered[chip * 2 + 1]]
        else:
            arrived(sibling, 2)
            own, other = packed[...], gathered[sibling]
            values = [jnp.where(core == 0, own, other), jnp.where(core == 0, other, own)]
        weights = jnp.concatenate(halves(jnp.concatenate(values, axis=0)), axis=0)
        lanes = pl.ds(pl.multiple_of(chip * WIDE, WIDE), WIDE)
        for dy, dz in ((1,1),(3,0),(2,1),(0,1),(1,0),(3,1),(2,0),(0,0)):
            q = (c // 4 + dy) % 4 * 2 + (c % 4 // 2 + dz) % 2
            both = dot(parts[q, :, lanes], weights, NT)
            both = both[0:CHUNK] + both[CHUNK:]
            if t:
                both += sums[q]
            if finish is None:
                sums[q] = both
            else:
                finish(q, both)

    lane = lax.broadcasted_iota(jnp.int32, (SHARE // 2, 128), 1)

    def finish(q, both):
        both = both + pltpu.roll(both, 2 * CAP, 1)
        for s in range(CHUNK // SHARE):
            to = q * 2 + s
            low = both[s * SHARE : s * SHARE + SHARE // 2]
            high = both[s * SHARE + SHARE // 2 : (s + 1) * SHARE]
            shares[to] = jnp.where(lane < 2 * CAP, low, high)

            @pl.when(to != c)
            def _():
                remote(shares.at[to], got.at[c], send.at[8], recv.at[8], r, to).start()

    accumulate(0)
    forward(1)
    forward(3)
    accumulate(1)
    forward(2)
    accumulate(3)
    accumulate(2, finish)
    own = pltpu.make_async_copy(shares.at[c], got.at[c], local_sem.at[3])
    own.start()
    own.wait()
    some = got.at[pl.ds(0, COLS - 1)]
    drain = remote(some, some, send.at[8], recv.at[8], r, c)
    drain.wait_recv()
    total = got[0]
    for k in range(1, COLS):
        total += got[k]

    ab_row = ab_ref[:, pl.ds(pl.multiple_of(c * SHARE, 128), SHARE)].astype(F32)
    hi, lo = halves(total)
    place = lax.broadcasted_iota(jnp.int32, (HALF, 128), 1).astype(F32)
    for g in range(2):
        slots = rank_col[g * HALF : (g + 1) * HALF] + float(g * CAP)
        pieces = []
        for h in range(2):
            pick = jnp.where(slots + float(h * 2 * CAP) == place, 1.0, 0.0).astype(BF16)
            pieces.append(dot(pick, hi, NT) + dot(pick, lo, NT))
        rows = jnp.where(key_col[g] == ab_row, jnp.concatenate(pieces, axis=1), 0.0)
        for i in range(2):
            fin[:, g, :, i, :] = rows[i * HALF // 2 : (i + 1) * HALF // 2].reshape(XS, COLS, 128)

    me = r * COLS + c

    for dx, dy, dz, dc in far_first((0, 1)):
        to_x, to_c, to_core = to_xs[dx], to_ys[dy] + to_zs[dz], to_cores[dc]
        remote(fin.at[to_x, to_core, to_c], out_ref.at[me], send.at[9], recv.at[9], to_x * 2 + to_core, to_c).start()
    own = pltpu.make_async_copy(fin.at[x, core, c], out_ref.at[me], local_sem.at[4])
    own.start()
    own.wait()
    drain.wait_send()
    some = out_ref.at[pl.ds(0, ROWS * COLS - 1)]
    handed = remote(some, some, send.at[9], recv.at[9], r, c)
    handed.wait_recv()
    handed.wait_send()
    given.wait_send()
    remote(packed, packed, send.at[2], recv.at[2], r, c).wait_send()
    three = gathered.at[pl.ds(0, 3)]
    remote(three, three, send.at[3], recv.at[2], r, c).wait_send()
    remote(three, three, send.at[7], recv.at[2], r, c).wait_send()


def packed_round(base, amps, integrals, ij_irrep, ab_irrep, cd_irrep):
    vmem = pl.BlockSpec(memory_space=pltpu.VMEM)
    hbm = pl.BlockSpec(memory_space=pl.ANY)
    out, most = pl.pallas_call(
        kernel,
        out_shape=(
            jax.ShapeDtypeStruct((ROWS * COLS, 2, 128), F32),
            jax.ShapeDtypeStruct((1, 1), jnp.int32),
        ),
        in_specs=[vmem, hbm, hbm, vmem, vmem, vmem],
        out_specs=(vmem, pl.BlockSpec(memory_space=pltpu.SMEM)),
        scratch_shapes=[
            pltpu.VMEM((BLOCK, BLOCK), F32),
            pltpu.VMEM((CHUNKS, 2 * CHUNK, BLOCK), BF16),
            pltpu.VMEM((BLOCK, 128), jnp.int32),
            pltpu.VMEM((XS * COLS, 8, 128), F32),
            pltpu.VMEM((CAP, WIDE), F32),
            pltpu.VMEM((ROWS, CAP, WIDE), F32),
            pltpu.VMEM((CHUNKS, CHUNK, 128), F32),
            pltpu.VMEM((COLS, SHARE // 2, 128), F32),
            pltpu.VMEM((COLS, SHARE // 2, 128), F32),
            pltpu.VMEM((XS, 2, COLS, 2, 128), F32),
            pltpu.SemaphoreType.DMA((CHUNKS,)),
            pltpu.SemaphoreType.DMA((6,)),
            pltpu.SemaphoreType.DMA((14,)),
            pltpu.SemaphoreType.DMA((14,)),
        ],
        compiler_params=pltpu.CompilerParams(collective_id=0, has_side_effects=True, vmem_limit_bytes=58 << 20),
        name="packed_round",
    )(base, amps, integrals, ij_irrep, ab_irrep, cd_irrep)
    return out.transpose(1, 0, 2).reshape(2, ROWS * COLS * 128), most


def body(amplitudes, integrals, ij_irrep, ab_irrep, cd_irrep):
    amps = amplitudes.reshape(2, COLS, XS, 4, 128).transpose(1, 2, 3, 0, 4).reshape(COLS, XS, 8, 128)
    rest = (amps, integrals, ij_irrep.reshape(1, -1), ab_irrep.reshape(1, -1), cd_irrep.reshape(1, -1))
    first = jnp.asarray(np.arange(128, dtype=np.int32)[None, :])
    out, most = packed_round(first, *rest)

    def more(state):
        return state[0] < most[0, 0]

    def another(state):
        base, so_far = state
        return base + CAP, so_far + packed_round(first + base, *rest)[0]

    _, out = lax.while_loop(more, another, (jnp.int32(CAP), out))
    return out


def solution(mesh):
    in_specs = (P(("row", "col"), None), P("row", "col"), P(), P("row"), P("col"))
    out_specs = P(("row", "col"), None)
    return jax.shard_map(body, mesh=mesh, in_specs=in_specs, out_specs=out_specs, check_vma=False)
```

```python
import jax
import jax.numpy as jnp
import numpy as np
from jax import lax
from jax.experimental import pallas as pl
from jax.experimental.pallas import tpu as pltpu
from jax.sharding import PartitionSpec as P

MESH = pl.DeviceIdType.MESH
ROWS, COLS = 8, 16
XS = 4
NIJ = 256
HALF = NIJ // 2
CAP = 32
BLOCK = 2048
WIDE = BLOCK // XS
CHUNKS = 8
CHUNK = BLOCK // CHUNKS
SHARE = BLOCK // COLS
F32, BF16 = jnp.float32, jnp.bfloat16
NT = (((1,), (1,)), ((), ()))


def dot(a, b, dims=(((1,), (0,)), ((), ()))):
    return lax.dot_general(a, b, dims, preferred_element_type=F32)


def halves(v):
    hi = v.astype(BF16)
    return hi, (v - hi.astype(F32)).astype(BF16)


def column(row):
    return jnp.transpose(jnp.broadcast_to(row, (128, 128)))


def remote(src, dst, send, recv, row, col):
    return pltpu.make_async_remote_copy(
        src_ref=src, dst_ref=dst, send_sem=send, recv_sem=recv, device_id=(row, col), device_id_type=MESH
    )


def kernel(
    base_ref, amp_ref, int_ref, ij_ref, ab_ref, cd_ref, out_ref, most_ref,
    ints, parts, ab_col, mine, packed, gathered, sums, shares, got, fin,
    int_sem, local_sem, send, recv,
):
    r, c = lax.axis_index("row"), lax.axis_index("col")
    x, core = r // 2, r % 2
    sibling = x * 2 + 1 - core

    def far_first(cores):
        near = lambda d: min(d, 4 - d)
        offsets = [(dx, dy, dz, dc) for dx in range(4) for dy in range(4) for dz in range(4) for dc in cores if dx or dy or dz or dc]
        return sorted(offsets, key=lambda o: -(near(o[0]) + near(o[1]) + near(o[2])))

    to_xs = [(x + d) % 4 for d in range(4)]
    to_ys = [(c // 4 + d) % 4 * 4 for d in range(4)]
    to_zs = [(c % 4 + d) % 4 for d in range(4)]
    to_cores = [core, 1 - core]

    barrier = pltpu.get_barrier_semaphore()
    place_of = x * COLS + c
    pl.semaphore_signal(barrier, inc=1, device_id=(sibling, c), device_id_type=MESH)

    for dx, dy, dz, dc in far_first((0,)):
        pl.semaphore_signal(barrier, inc=1, device_id=(to_xs[dx] * 2 + core, to_ys[dy] + to_zs[dz]), device_id_type=MESH)
    def fetch(q):
        rows = pl.ds(q * CHUNK, CHUNK)
        return pltpu.make_async_copy(int_ref.at[rows], ints.at[rows], int_sem.at[q])

    for q in range(CHUNKS):
        fetch(q).start()

    ij_row = jnp.broadcast_to(ij_ref[...], (8, NIJ)).astype(F32).astype(BF16)
    source = lax.broadcasted_iota(jnp.int32, (NIJ, NIJ), 0)
    target = lax.broadcasted_iota(jnp.int32, (NIJ, NIJ), 1)
    wanted = (target // 16 % 4) * 64 + (target // 128) * 32 + (target % 16) * 2 + (target // 64 % 2)
    reorder = jnp.where(source == wanted, 1.0, 0.0).astype(F32).astype(BF16)
    key_row = dot(ij_row, reorder)[0:1, :]
    key_col = [column(key_row[:, 0:HALF]), column(key_row[:, HALF:NIJ])]
    keys = jnp.concatenate(key_col, axis=0)
    keys = jnp.concatenate([keys, keys], axis=1)
    same = (keys == key_row) & (source // HALF == target // HALF)
    rank_row = jnp.sum(jnp.where(same & (source < target), 1.0, 0.0), axis=0, keepdims=True)
    rank_col = jnp.sum(jnp.where(same & (target < source), 1.0, 0.0), axis=1, keepdims=True)
    most_ref[0, 0] = jnp.max(rank_row).astype(jnp.int32) + 1
    base = base_ref[...].astype(F32)
    rank_row = rank_row - base[0:1, 0:1]
    rank_col = rank_col - base[0:1, 0:1]
    rank_col = jnp.where((rank_col >= 0.0) & (rank_col < float(CAP)), rank_col, -4.0 * NIJ)

    for q in range(COLS):
        ab_col[pl.ds(q * 128, 128), :] = column(ab_ref[:, pl.ds(q * 128, 128)])

    def prepare(first, last):
        for q in range(first, last):
            fetch(q).wait()

            def step(s, carry, q=q):
                rows = pl.ds(pl.multiple_of(q * CHUNK + s * 16, 16), 16)
                label = ab_col[rows, :]
                for j in range(BLOCK // 128):
                    lanes = pl.ds(j * 128, 128)
                    value = jnp.where(label == cd_ref[:, lanes], ints[rows, lanes], 0.0)
                    hi, lo = halves(value)
                    at = pl.ds(pl.multiple_of(s * 16, 16), 16)
                    parts[q, at, lanes] = hi
                    parts[q, pl.ds(pl.multiple_of(CHUNK + s * 16, 16), 16), lanes] = lo
                return carry

            lax.fori_loop(0, CHUNK // 16, step, 0)

    prepare(0, 2)
    pl.semaphore_wait(barrier, XS * COLS)

    for dx, dy, dz, dc in far_first((0,)):
        to_x, to_c = to_xs[dx], to_ys[dy] + to_zs[dz]
        remote(amp_ref.at[to_c, to_x], mine.at[place_of], send.at[0], recv.at[0], to_x * 2 + core, to_c).start()
    own = pltpu.make_async_copy(amp_ref.at[c, x], mine.at[place_of], local_sem.at[0])
    own.start()
    prepare(2, 7)
    own.wait()

    some = mine.at[pl.ds(0, XS * COLS - 1)]
    given = remote(some, some, send.at[0], recv.at[0], r, c)
    given.wait_recv()

    slot = lax.broadcasted_iota(jnp.int32, (CAP, HALF), 0).astype(F32)
    my_rank = jnp.where(core == 0, rank_row[:, 0:HALF], rank_row[:, HALF:NIJ])
    my_key = jnp.where(core == 0, key_col[0], key_col[1])
    pick = jnp.where(my_rank == slot, 1.0, 0.0).astype(BF16)
    for t in range(WIDE // 128):
        cd_row = cd_ref[:, pl.ds(pl.multiple_of(x * WIDE + t * 128, 128), 128)].astype(F32)
        amps = jnp.concatenate([mine[:, t * 2 + i, :] for i in range(2)], axis=0)
        hi, lo = halves(jnp.where(my_key == cd_row, amps, 0.0))
        packed[:, t * 128 : (t + 1) * 128] = dot(pick, hi) + dot(pick, lo)

    for t in (1, 3, 2):
        remote(packed, gathered.at[r], send.at[3], recv.at[3 + t], (x + t) % 4 * 2 + core, c).start()
    remote(packed, gathered.at[r], send.at[2], recv.at[2], sibling, c).start()

    def arrived(k, sem):
        remote(gathered.at[k], gathered.at[k], send.at[3], recv.at[sem], r, c).wait_recv()

    def forward(t):
        k = (x + 4 - t) % 4 * 2 + core
        arrived(k, 3 + t)
        remote(gathered.at[k], gathered.at[k], send.at[7], recv.at[10 + t], sibling, c).start()

    def accumulate(t, finish=None):
        chip = (x + 4 - t) % 4
        if t:
            arrived(chip * 2 + 1 - core, 10 + t)
            values = [gathered[chip * 2], gathered[chip * 2 + 1]]
        else:
            arrived(sibling, 2)
            own, other = packed[...], gathered[sibling]
            values = [jnp.where(core == 0, own, other), jnp.where(core == 0, other, own)]
        weights = jnp.concatenate(halves(jnp.concatenate(values, axis=0)), axis=0)
        lanes = pl.ds(pl.multiple_of(chip * WIDE, WIDE), WIDE)
        for dy, dz in ((1,1),(3,0),(2,1),(0,1),(1,0),(3,1),(2,0),(0,0)):
            q = (c // 4 + dy) % 4 * 2 + (c % 4 // 2 + dz) % 2
            both = dot(parts[q, :, lanes], weights, NT)
            both = both[0:CHUNK] + both[CHUNK:]
            if t:
                both += sums[q]
            if finish is None:
                sums[q] = both
            else:
                finish(q, both)

    lane = lax.broadcasted_iota(jnp.int32, (SHARE // 2, 128), 1)

    def finish(q, both):
        both = both + pltpu.roll(both, 2 * CAP, 1)
        for s in range(CHUNK // SHARE):
            to = q * 2 + s
            low = both[s * SHARE : s * SHARE + SHARE // 2]
            high = both[s * SHARE + SHARE // 2 : (s + 1) * SHARE]
            shares[to] = jnp.where(lane < 2 * CAP, low, high)

            @pl.when(to != c)
            def _():
                remote(shares.at[to], got.at[c], send.at[8], recv.at[8], r, to).start()

    prepare(7, 8)
    accumulate(0)
    forward(1)
    forward(3)
    accumulate(1)
    forward(2)
    accumulate(3)
    accumulate(2, finish)
    own = pltpu.make_async_copy(shares.at[c], got.at[c], local_sem.at[3])
    own.start()
    own.wait()
    some = got.at[pl.ds(0, COLS - 1)]
    drain = remote(some, some, send.at[8], recv.at[8], r, c)
    drain.wait_recv()
    total = got[0]
    for k in range(1, COLS):
        total += got[k]

    ab_row = ab_ref[:, pl.ds(pl.multiple_of(c * SHARE, 128), SHARE)].astype(F32)
    hi, lo = halves(total)
    place = lax.broadcasted_iota(jnp.int32, (HALF, 128), 1).astype(F32)
    for g in range(2):
        slots = rank_col[g * HALF : (g + 1) * HALF] + float(g * CAP)
        pieces = []
        for h in range(2):
            pick = jnp.where(slots + float(h * 2 * CAP) == place, 1.0, 0.0).astype(BF16)
            pieces.append(dot(pick, hi, NT) + dot(pick, lo, NT))
        rows = jnp.where(key_col[g] == ab_row, jnp.concatenate(pieces, axis=1), 0.0)
        for i in range(2):
            fin[:, g, :, i, :] = rows[i * HALF // 2 : (i + 1) * HALF // 2].reshape(XS, COLS, 128)

    me = r * COLS + c

    for dx, dy, dz, dc in far_first((0, 1)):
        to_x, to_c, to_core = to_xs[dx], to_ys[dy] + to_zs[dz], to_cores[dc]
        remote(fin.at[to_x, to_core, to_c], out_ref.at[me], send.at[9], recv.at[9], to_x * 2 + to_core, to_c).start()
    own = pltpu.make_async_copy(fin.at[x, core, c], out_ref.at[me], local_sem.at[4])
    own.start()
    own.wait()
    drain.wait_send()
    some = out_ref.at[pl.ds(0, ROWS * COLS - 1)]
    handed = remote(some, some, send.at[9], recv.at[9], r, c)
    handed.wait_recv()
    handed.wait_send()
    given.wait_send()
    remote(packed, packed, send.at[2], recv.at[2], r, c).wait_send()
    three = gathered.at[pl.ds(0, 3)]
    remote(three, three, send.at[3], recv.at[2], r, c).wait_send()
    remote(three, three, send.at[7], recv.at[2], r, c).wait_send()


def packed_round(base, amps, integrals, ij_irrep, ab_irrep, cd_irrep):
    vmem = pl.BlockSpec(memory_space=pltpu.VMEM)
    hbm = pl.BlockSpec(memory_space=pl.ANY)
    out, most = pl.pallas_call(
        kernel,
        out_shape=(
            jax.ShapeDtypeStruct((ROWS * COLS, 2, 128), F32),
            jax.ShapeDtypeStruct((1, 1), jnp.int32),
        ),
        in_specs=[vmem, hbm, hbm, vmem, vmem, vmem],
        out_specs=(vmem, pl.BlockSpec(memory_space=pltpu.SMEM)),
        scratch_shapes=[
            pltpu.VMEM((BLOCK, BLOCK), F32),
            pltpu.VMEM((CHUNKS, 2 * CHUNK, BLOCK), BF16),
            pltpu.VMEM((BLOCK, 128), jnp.int32),
            pltpu.VMEM((XS * COLS, 8, 128), F32),
            pltpu.VMEM((CAP, WIDE), F32),
            pltpu.VMEM((ROWS, CAP, WIDE), F32),
            pltpu.VMEM((CHUNKS, CHUNK, 128), F32),
            pltpu.VMEM((COLS, SHARE // 2, 128), F32),
            pltpu.VMEM((COLS, SHARE // 2, 128), F32),
            pltpu.VMEM((XS, 2, COLS, 2, 128), F32),
            pltpu.SemaphoreType.DMA((CHUNKS,)),
            pltpu.SemaphoreType.DMA((6,)),
            pltpu.SemaphoreType.DMA((14,)),
            pltpu.SemaphoreType.DMA((14,)),
        ],
        compiler_params=pltpu.CompilerParams(collective_id=0, has_side_effects=True, vmem_limit_bytes=58 << 20),
        name="packed_round",
    )(base, amps, integrals, ij_irrep, ab_irrep, cd_irrep)
    return out.transpose(1, 0, 2).reshape(2, ROWS * COLS * 128), most


def body(amplitudes, integrals, ij_irrep, ab_irrep, cd_irrep):
    amps = amplitudes.reshape(2, COLS, XS, 4, 128).transpose(1, 2, 3, 0, 4).reshape(COLS, XS, 8, 128)
    rest = (amps, integrals, ij_irrep.reshape(1, -1), ab_irrep.reshape(1, -1), cd_irrep.reshape(1, -1))
    first = jnp.asarray(np.arange(128, dtype=np.int32)[None, :])
    out, most = packed_round(first, *rest)

    def more(state):
        return state[0] < most[0, 0]

    def another(state):
        base, so_far = state
        return base + CAP, so_far + packed_round(first + base, *rest)[0]

    _, out = lax.while_loop(more, another, (jnp.int32(CAP), out))
    return out


def solution(mesh):
    in_specs = (P(("row", "col"), None), P("row", "col"), P(), P("row"), P("col"))
    out_specs = P(("row", "col"), None)
    return jax.shard_map(body, mesh=mesh, in_specs=in_specs, out_specs=out_specs, check_vma=False)
```
